32 devices in a mesh: parts: 2 (over x), obs: 16 (over z, y, core).
Axes of the slice: x: 2, y: 2, z: 4, core: 2. Of those that a mesh axis runs over, the one named last changes fastest.
Arguments:
- theta: bfloat16 [1024, 24576], P(None, ('parts', 'obs')), parts along dimension 1, may hold values from -6 to 6
- predictions: bfloat16 [1024, 8192], P(None, ('parts', 'obs')), parts along dimension 1, may hold values from -6 to 6
- perturb: bfloat16 [1024, 8192], P(None, ('parts', 'obs')), parts along dimension 1, may hold values from -6 to 6
- obs_value: float32 [8192], P(('parts', 'obs')), parts along dimension 0, may hold values from -6 to 6
- obs_prec: float32 [8192], P(('parts', 'obs')), parts along dimension 0, may hold values from 0.3 to 3
- pattern: int32 [96, 8], P(('parts', 'obs')), parts along dimension 0, may hold values from 0 to 16, as said below
- obs_count: int32 [32], P('parts'), parts along dimension 0, may hold values from 64 to 256, as said below
Outputs:
- theta_new: bfloat16 [1024, 24576], P(None, ('parts', 'obs')), parts along dimension 1
The draws below stay inside these ranges and needn't reach their ends.
There are 2 independent parts, one for each index of `parts`. The reference program is written for one: setup_inputs(seed, part) draws one part's arguments, and reference() takes and returns one part's arrays. A program takes and returns all parts, laid end to end along the dimension named above; each array names one. Nothing has to cross between parts.
Inputs may be any that keep to these rules, and one draw needn't show every extreme that they name: `pattern`: each row names one to 8 distinct observation blocks, the rest of its slots hold 16; some row names exactly 8. `obs_count`: some block uses all 256 slots.
All inputs are finite; a program needn't handle non-finite values.
Results may differ from the reference program's by a relative error of at most 0.0043.
Values may be sent and summed in bfloat16 or wider, within the bound.
A program may use at most 192 MiB of HBM per device.

```python
import math
import jax
import jax.numpy as jnp
from jax import lax

MEMBERS = 1024
BLK = 256
KMAX = 8
PBLOCKS = 48
OBLOCKS = 16
PARAMS = 12288
OBSERV = 4096


def draw_pattern(key, part):
    key = jax.random.fold_in(key, 11)
    key_count, key_rows = jax.random.split(key)
    row_counts = jax.random.randint(key_count, (PBLOCKS,), 1, KMAX + 1).astype(jnp.int32)
    row_counts = row_counts.at[0].set(KMAX)
    row_keys = jax.random.split(key_rows, PBLOCKS)

    def one_row(row_key):
        return jax.random.permutation(row_key, OBLOCKS)[:KMAX].astype(jnp.int32)
    chosen = jax.vmap(one_row)(row_keys)
    slots = jnp.arange(KMAX, dtype=jnp.int32)
    return jnp.where(slots[None, :] < row_counts[:, None], chosen, OBLOCKS).astype(jnp.int32)


def draw_obs_count(key, part):
    key = jax.random.fold_in(key, 23)
    blocks = jnp.arange(OBLOCKS, dtype=jnp.int32)
    lowest = BLK // 4 + 3 * BLK // 4 * blocks // OBLOCKS
    counts = jax.random.randint(key, (OBLOCKS,), lowest, BLK + 1).astype(jnp.int32)
    return counts.at[OBLOCKS - 1].set(BLK)


def shard_levels(stream_key, dims, cuts, smallest, largest):
    level = 1.0
    for position, parts in cuts:
        draws = jax.random.uniform(jax.random.fold_in(jax.random.fold_in(stream_key, 6), position), (parts,), jnp.float32, smallest / len(cuts), largest / len(cuts))
        level = level * jnp.repeat(jnp.exp(draws), dims[position] // parts).reshape((-1,) + (1,) * (len(dims) - 1 - position))
    return level


def noise(stream_key, extent, spread, reach, cuts=(), kind=jnp.bfloat16):
    result = jax.random.normal(stream_key, extent, jnp.float32) * spread
    if len(cuts) > 0:
        result = shard_levels(stream_key, extent, cuts, -0.22, 0.18) * result
    return jnp.clip(result, min=-reach, max=reach).astype(kind)


def setup_inputs(seed: int = 0, part: int = 0) -> dict:
    keys = jax.random.split(jax.random.key(seed), 8)
    part_splits = jax.random.split(jax.random.fold_in(keys[7], part), 8)
    return {
        "theta": noise(part_splits[0], (MEMBERS, PARAMS), 1.0, 6.0, ((1, 16),)),
        "predictions": noise(part_splits[1], (MEMBERS, OBSERV), 1.0, 6.0, ((1, 16),)),
        "perturb": noise(part_splits[2], (MEMBERS, OBSERV), 1.0, 6.0, ((1, 16),)),
        "obs_value": noise(part_splits[3], (OBSERV,), 1.0, 6.0, ((0, 16),), jnp.float32),
        "obs_prec": jnp.clip(jnp.exp(math.log(3.0) - 2.3025851 * jax.random.uniform(part_splits[4], (OBSERV,), jnp.float32) ** shard_levels(part_splits[4], (OBSERV,), ((0, 16),), -0.2, 0.2)), 0.3, 3.0),
        "pattern": draw_pattern(jax.random.fold_in(jax.random.fold_in(keys[7], part), 71), part),
        "obs_count": draw_obs_count(jax.random.fold_in(jax.random.fold_in(keys[7], part), 71), part),
    }


def reference(theta, predictions, perturb, obs_value, obs_prec, pattern, obs_count):
    theta_f = theta.astype(jnp.float32)
    theta_anom = (theta_f - lax.optimization_barrier(jnp.mean(theta_f, axis=0, keepdims=True))).astype(jnp.bfloat16)
    pred_f = predictions.astype(jnp.float32)
    pred_anom = (pred_f - lax.optimization_barrier(jnp.mean(pred_f, axis=0, keepdims=True))).astype(jnp.bfloat16)
    column = jnp.arange(OBSERV, dtype=jnp.int32)
    usable = (column % BLK < obs_count[column // BLK]).astype(jnp.float32)
    innovation = (usable * (obs_prec[None, :] * (obs_value[None, :] - pred_f) + jnp.sqrt(obs_prec)[None, :] * perturb.astype(jnp.float32))).astype(jnp.bfloat16)
    misfit = jnp.sum(jnp.square(innovation.astype(jnp.float32)))
    obs_total = jnp.sum(obs_count).astype(jnp.float32)
    step_size = 1.0 / (1.0 + misfit / (MEMBERS * obs_total))

    def one_block(param_slot):
        own_block = lax.dynamic_slice_in_dim(theta_anom, (param_slot * BLK).astype(jnp.int32), BLK, 1)

        def visit(summed, linked):

            def add_pair(current):
                offset = (linked * BLK).astype(jnp.int32)
                pred_block = lax.dynamic_slice_in_dim(pred_anom, offset, BLK, 1)
                innov_block = lax.dynamic_slice_in_dim(innovation, offset, BLK, 1)
                cross = jnp.dot(pred_block.T, own_block, preferred_element_type=jnp.float32).astype(jnp.bfloat16)
                return current + jnp.dot(innov_block, cross, preferred_element_type=jnp.float32)

            def keep_pair(current):
                return current
            return (lax.cond(linked < OBLOCKS, add_pair, keep_pair, summed), None)
        summed, unused = lax.scan(visit, jnp.zeros((MEMBERS, BLK), jnp.float32), pattern[param_slot])
        return summed
    blocks = lax.map(one_block, jnp.arange(PBLOCKS, dtype=jnp.int32))
    update = jnp.transpose(blocks, (1, 0, 2)).reshape(MEMBERS, PARAMS)
    return (theta_f + step_size / (MEMBERS - 1) * update).astype(jnp.bfloat16)
```

```python
import functools
import jax
import jax.numpy as jnp
from jax import lax
from jax.experimental import pallas as pl
from jax.experimental.pallas import tpu as pltpu
from jax.sharding import PartitionSpec as P

MESH = pl.DeviceIdType.MESH
F32 = jnp.float32
BF16 = jnp.bfloat16
PRED_PIECES = 2
CHUNKS = 8
AHEAD = 3


def kernel(
    nz,
    theta_ref, pred_ref, pert_ref, val_ref, prec_ref, patt_ref, count_ref,
    out_ref,
    th, pall, iall, cross, own_sum, psend, precv, mask, mis,
    ps, pr, isd, ir, ts, tr, ks, kr, ms, mr, us, ur,
):
    members, width = theta_ref.shape
    blk = pred_ref.shape[1]
    groups = width // blk
    nobs = nz * 4
    rp = blk // PRED_PIECES
    rk = members // CHUNKS
    part = lax.axis_index("parts")
    me = lax.axis_index("obs")
    z = me // 4
    y = (me // 2) % 2
    c = me % 2

    def dev(zz, yy, cc):
        return (part, zz * 4 + yy * 2 + cc)

    sib = dev(z, y, 1 - c)
    mate = dev(z, 1 - y, c)

    barrier = pltpu.get_barrier_semaphore()
    pl.semaphore_signal(barrier, inc=1, device_id=sib, device_id_type=MESH)
    pl.semaphore_signal(barrier, inc=1, device_id=mate, device_id_type=MESH)
    for h in range(1, nz):
        pl.semaphore_signal(
            barrier, inc=1, device_id=dev((z + h) % nz, y, c), device_id_type=MESH
        )

    def target(d):
        return (dev(z + 1, y, c), dev(z - 1, y, c), sib)[d]

    def pcopy(zz, cc, p, d):
        r = pall.at[pl.ds(pl.multiple_of((zz * 2 + cc) * blk + p * rp, rp), rp), :]
        return pltpu.make_async_remote_copy(
            src_ref=r, dst_ref=r, send_sem=ps.at[d, p, zz], recv_sem=pr.at[p, zz * 2 + cc],
            device_id=target(d), device_id_type=MESH,
        )

    def icopy(zz, cc, k, d):
        r = iall.at[
            pl.ds(pl.multiple_of(k * rk, rk), rk),
            pl.ds(pl.multiple_of((zz * 2 + cc) * blk, blk), blk),
        ]
        return pltpu.make_async_remote_copy(
            src_ref=r, dst_ref=r, send_sem=isd.at[d, k, zz], recv_sem=ir.at[k, zz * 2 + cc],
            device_id=target(d), device_id_type=MESH,
        )

    def send_own(copy, p):
        @pl.when(z + 1 < nz)
        def _():
            copy(z, c, p, 0).start()

        @pl.when(z >= 1)
        def _():
            copy(z, c, p, 1).start()

    def relay(copy, s, p):
        below = z - 1 - s
        above = z + 1 + s

        @pl.when(below >= 0)
        def _():
            copy(below, c, p, 2).wait_recv()

            @pl.when(z + 1 < nz)
            def _():
                copy(below, c, p, 0).start()

            copy(below, c, p, 2).start()

        @pl.when(above < nz)
        def _():
            copy(above, c, p, 2).wait_recv()

            @pl.when(z >= 1)
            def _():
                copy(above, c, p, 1).start()

            copy(above, c, p, 2).start()

    def tcopy(t):
        return pltpu.make_async_remote_copy(
            src_ref=th.at[0, t], dst_ref=th.at[1, t], send_sem=ts.at[t], recv_sem=tr.at[t],
            device_id=mate, device_id_type=MESH,
        )

    kcopy = pltpu.make_async_remote_copy(
        src_ref=mask.at[0], dst_ref=mask.at[1], send_sem=ks, recv_sem=kr,
        device_id=mate, device_id_type=MESH,
    )

    def ucopy(k):
        rows = pl.ds(pl.multiple_of(k * rk, rk), rk)
        return pltpu.make_async_remote_copy(
            src_ref=psend.at[rows, :], dst_ref=precv.at[rows, :],
            send_sem=us.at[k], recv_sem=ur.at[k], device_id=mate, device_id_type=MESH,
        )

    def mcopy(src, dst, sem, device):
        return pltpu.make_async_remote_copy(
            src_ref=mis.at[src], dst_ref=mis.at[dst], send_sem=ms.at[sem], recv_sem=mr.at[dst],
            device_id=device, device_id_type=MESH,
        )

    pred_f = pred_ref[...].astype(F32)
    anom = pred_f - jnp.mean(pred_f, axis=0, keepdims=True)
    own_slot = z * 2 + c
    pall[pl.ds(pl.multiple_of(own_slot * blk, blk), blk), :] = anom.T.astype(BF16)

    pl.semaphore_wait(barrier, nz + 1)
    for p in range(PRED_PIECES):
        send_own(pcopy, p)
    for t in range(groups):
        x = theta_ref[:, t * blk:(t + 1) * blk].astype(F32)
        th[0, t] = (x - jnp.mean(x, axis=0, keepdims=True)).astype(BF16)
        tcopy(t).start()
    for p in range(PRED_PIECES):
        pcopy(z, c, p, 2).start()

    block_of_row = lax.broadcasted_iota(jnp.int32, (nobs, blk), 0)
    for t in range(groups):
        hit = jnp.zeros((nobs, blk), F32)
        for slot in range(patt_ref.shape[1]):
            hit = jnp.where(block_of_row == patt_ref[t:t + 1, slot:slot + 1], 1.0, hit)
        mask[0, :, t * blk:(t + 1) * blk] = hit
    kcopy.start()

    column = lax.broadcasted_iota(jnp.int32, (1, blk), 1)
    usable = (column < count_ref[me]).astype(F32)
    prec = prec_ref[...]
    innov = (
        usable
        * (
            prec * (val_ref[...] - pred_ref[...].astype(F32))
            + jnp.sqrt(prec) * pert_ref[...].astype(F32)
        )
    ).astype(BF16)
    iall[:, pl.ds(pl.multiple_of(own_slot * blk, blk), blk)] = innov
    for k in range(AHEAD):
        send_own(icopy, k)
    for k in range(CHUNKS):
        icopy(z, c, k, 2).start()
    squares = jnp.square(innov.astype(F32))
    mis[0] = jnp.sum(squares.reshape(members // 8, 8, blk), axis=0)
    mcopy(0, 1, 0, sib).start()

    def cross_pair(slot, which, t):
        linked = mask[which, pl.ds((slot // 2) * 4 + y * 2 + slot % 2, 1), t * blk:(t + 1) * blk]
        rows = pl.ds(pl.multiple_of(slot * blk, blk), blk)
        found = jnp.dot(pall[rows, :], th[which, t], preferred_element_type=F32)
        at = (which * groups + t) * blk
        cross[rows, at:at + blk] = (found * linked).astype(BF16)

    def cross_own(zz):
        for p in range(PRED_PIECES):
            pcopy(zz, 1 - c, p, 2).wait_recv()

        def one(cc, _):
            for t in range(groups):
                cross_pair(zz * 2 + cc, 0, t)
            return 0

        lax.fori_loop(0, 2, one, 0)

    cross_own(z)
    for s in range(nz - 1):
        for p in range(PRED_PIECES):
            relay(pcopy, s, p)

        @pl.when(z - 1 - s >= 0)
        def _():
            cross_own(z - 1 - s)

        @pl.when(z + 1 + s < nz)
        def _():
            cross_own(z + 1 + s)

        if s == 0:
            mcopy(0, 1, 0, sib).wait_recv()
            mis[2] = mis[0] + mis[1]
            mcopy(2, 3, 1, mate).start()
        if s == 1:
            mcopy(2, 3, 1, mate).wait_recv()
            mis[4 + z] = mis[2] + mis[3]
            for h in range(1, nz):
                mcopy(4 + z, 4 + z, 1 + h, dev((z + h) % nz, y, c)).start()

    kcopy.wait_recv()
    for t in range(groups):
        tcopy(t).wait_recv()

    def mate_cross(slot, _):
        for t in range(groups):
            cross_pair(slot, 1, t)
        return 0

    lax.fori_loop(0, nz * 2, mate_cross, 0)

    for h in range(1, nz):
        other = (z + h) % nz
        mcopy(4 + other, 4 + other, 1 + h, dev(other, y, c)).wait_recv()
    tile = mis[4]
    for zz in range(1, nz):
        tile = tile + mis[4 + zz]
    misfit = jnp.sum(jnp.sum(tile, axis=0, keepdims=True), axis=1, keepdims=True)
    total = count_ref[0]
    for b in range(1, nobs):
        total = total + count_ref[b]
    scale = 1.0 / (1.0 + misfit / (members * total.astype(F32))) / (members - 1)

    def finish(k):
        ucopy(k).wait_recv()
        rows = pl.ds(pl.multiple_of(k * rk, rk), rk)
        update = own_sum[rows, :] + precv[rows, :].astype(F32)
        out_ref[rows, :] = (theta_ref[rows, :].astype(F32) + scale * update).astype(BF16)

    def chunk(k, _):
        @pl.when(k + AHEAD < CHUNKS)
        def _():
            send_own(icopy, k + AHEAD)

        for s in range(nz - 1):
            relay(icopy, s, k)
        for zz in range(nz):
            icopy(zz, 1 - c, k, 2).wait_recv()
        rows = pl.ds(pl.multiple_of(k * rk, rk), rk)
        psend[rows, :] = jnp.dot(
            iall[rows, :], cross[:, width:], preferred_element_type=F32
        ).astype(BF16)
        ucopy(k).start()
        own_sum[rows, :] = jnp.dot(
            iall[rows, :], cross[:, :width], preferred_element_type=F32
        )

        @pl.when(k >= 2)
        def _():
            finish(k - 2)

        return 0

    lax.fori_loop(0, CHUNKS, chunk, 0)
    finish(CHUNKS - 2)
    finish(CHUNKS - 1)

    def drain(copy, p):
        for zz in range(nz):
            @pl.when((z + 1 < nz) & (z >= zz))
            def _():
                copy(zz, c, p, 0).wait_send()

            @pl.when((z >= 1) & (z <= zz))
            def _():
                copy(zz, c, p, 1).wait_send()

            copy(zz, c, p, 2).wait_send()

    for p in range(PRED_PIECES):
        drain(pcopy, p)

    def drain_chunk(k, _):
        drain(icopy, k)
        ucopy(k).wait_send()
        return 0

    lax.fori_loop(0, CHUNKS, drain_chunk, 0)
    for t in range(groups):
        tcopy(t).wait_send()
    kcopy.wait_send()
    mcopy(0, 1, 0, sib).wait_send()
    mcopy(2, 3, 1, mate).wait_send()
    for h in range(1, nz):
        mcopy(4 + z, 4 + z, 1 + h, dev((z + h) % nz, y, c)).wait_send()


def body(theta, predictions, perturb, obs_value, obs_prec, pattern, obs_count):
    members, width = theta.shape
    blk = predictions.shape[1]
    groups = width // blk
    nobs = lax.axis_size("obs")
    nz = nobs // 4
    row = nz * 2
    dma = pltpu.SemaphoreType.DMA
    vmem = pl.BlockSpec(memory_space=pltpu.VMEM)
    return pl.pallas_call(
        functools.partial(kernel, nz),
        out_shape=jax.ShapeDtypeStruct((members, width), BF16),
        in_specs=[vmem] * 6 + [pl.BlockSpec(memory_space=pltpu.SMEM)],
        out_specs=vmem,
        scratch_shapes=[
            pltpu.VMEM((2, groups, members, blk), BF16),
            pltpu.VMEM((row * blk, members), BF16),
            pltpu.VMEM((members, row * blk), BF16),
            pltpu.VMEM((row * blk, 2 * width), BF16),
            pltpu.VMEM((members, width), F32),
            pltpu.VMEM((members, width), BF16),
            pltpu.VMEM((members, width), BF16),
            pltpu.VMEM((2, nobs, width), F32),
            pltpu.VMEM((4 + nz, 8, blk), F32),
            dma((3, PRED_PIECES, nz)),
            dma((PRED_PIECES, row)),
            dma((3, CHUNKS, nz)),
            dma((CHUNKS, row)),
            dma((groups,)),
            dma((groups,)),
            dma(()),
            dma(()),
            dma((1 + nz,)),
            dma((4 + nz,)),
            dma((CHUNKS,)),
            dma((CHUNKS,)),
        ],
        compiler_params=pltpu.CompilerParams(
            collective_id=0, has_side_effects=True, vmem_limit_bytes=58 * 1024 * 1024
        ),
        cost_estimate=pl.CostEstimate(
            flops=4 * members * nobs * blk * width,
            bytes_accessed=2 * members * (2 * width + 2 * blk),
            transcendentals=0,
        ),
    )(
        theta, predictions, perturb,
        obs_value.reshape(1, blk), obs_prec.reshape(1, blk), pattern, obs_count,
    )


def solution(mesh):
    return jax.shard_map(
        body,
        mesh=mesh,
        in_specs=(
            P(None, ("parts", "obs")),
            P(None, ("parts", "obs")),
            P(None, ("parts", "obs")),
            P(("parts", "obs")),
            P(("parts", "obs")),
            P(("parts", "obs"), None),
            P("parts"),
        ),
        out_specs=P(None, ("parts", "obs")),
        check_vma=False,
    )
```

```python
import functools
import jax
import jax.numpy as jnp
from jax import lax
from jax.experimental import pallas as pl
from jax.experimental.pallas import tpu as pltpu
from jax.sharding import PartitionSpec as P

MESH = pl.DeviceIdType.MESH
F32 = jnp.float32
BF16 = jnp.bfloat16
PRED_PIECES = 2
CHUNKS = 4
AHEAD = 2


def kernel(
    nz,
    theta_ref, pred_ref, pert_ref, val_ref, prec_ref, patt_ref, count_ref,
    out_ref,
    th, pall, iall, cross, own_sum, psend, precv, mask, mis,
    ps, pr, isd, ir, ts, tr, ks, kr, ms, mr, us, ur,
):
    members, width = theta_ref.shape
    blk = pred_ref.shape[1]
    groups = width // blk
    nobs = nz * 4
    rp = blk // PRED_PIECES
    rk = members // CHUNKS
    part = lax.axis_index("parts")
    me = lax.axis_index("obs")
    z = me // 4
    y = (me // 2) % 2
    c = me % 2

    def dev(zz, yy, cc):
        return (part, zz * 4 + yy * 2 + cc)

    sib = dev(z, y, 1 - c)
    mate = dev(z, 1 - y, c)

    barrier = pltpu.get_barrier_semaphore()
    pl.semaphore_signal(barrier, inc=1, device_id=sib, device_id_type=MESH)
    pl.semaphore_signal(barrier, inc=1, device_id=mate, device_id_type=MESH)
    for h in range(1, nz):
        pl.semaphore_signal(
            barrier, inc=1, device_id=dev((z + h) % nz, y, c), device_id_type=MESH
        )

    def target(d):
        return (dev(z + 1, y, c), dev(z - 1, y, c), sib)[d]

    def pcopy(zz, cc, p, d):
        r = pall.at[pl.ds(pl.multiple_of((zz * 2 + cc) * blk + p * rp, rp), rp), :]
        return pltpu.make_async_remote_copy(
            src_ref=r, dst_ref=r, send_sem=ps.at[d, p, zz], recv_sem=pr.at[p, zz * 2 + cc],
            device_id=target(d), device_id_type=MESH,
        )

    def icopy(zz, cc, k, d):
        r = iall.at[
            pl.ds(pl.multiple_of(k * rk, rk), rk),
            pl.ds(pl.multiple_of((zz * 2 + cc) * blk, blk), blk),
        ]
        return pltpu.make_async_remote_copy(
            src_ref=r, dst_ref=r, send_sem=isd.at[d, k, zz], recv_sem=ir.at[k, zz * 2 + cc],
            device_id=target(d), device_id_type=MESH,
        )

    def send_own(copy, p):
        @pl.when(z + 1 < nz)
        def _():
            copy(z, c, p, 0).start()

        @pl.when(z >= 1)
        def _():
            copy(z, c, p, 1).start()

    def relay(copy, s, p):
        below = z - 1 - s
        above = z + 1 + s

        @pl.when(below >= 0)
        def _():
            copy(below, c, p, 2).wait_recv()

            @pl.when(z + 1 < nz)
            def _():
                copy(below, c, p, 0).start()

            copy(below, c, p, 2).start()

        @pl.when(above < nz)
        def _():
            copy(above, c, p, 2).wait_recv()

            @pl.when(z >= 1)
            def _():
                copy(above, c, p, 1).start()

            copy(above, c, p, 2).start()

    def tcopy(t):
        return pltpu.make_async_remote_copy(
            src_ref=th.at[0, t], dst_ref=th.at[1, t], send_sem=ts.at[t], recv_sem=tr.at[t],
            device_id=mate, device_id_type=MESH,
        )

    kcopy = pltpu.make_async_remote_copy(
        src_ref=mask.at[0], dst_ref=mask.at[1], send_sem=ks, recv_sem=kr,
        device_id=mate, device_id_type=MESH,
    )

    def ucopy(k):
        rows = pl.ds(pl.multiple_of(k * rk, rk), rk)
        return pltpu.make_async_remote_copy(
            src_ref=psend.at[rows, :], dst_ref=precv.at[rows, :],
            send_sem=us.at[k], recv_sem=ur.at[k], device_id=mate, device_id_type=MESH,
        )

    def mcopy(src, dst, sem, device):
        return pltpu.make_async_remote_copy(
            src_ref=mis.at[src], dst_ref=mis.at[dst], send_sem=ms.at[sem], recv_sem=mr.at[dst],
            device_id=device, device_id_type=MESH,
        )

    pred_f = pred_ref[...].astype(F32)
    anom = pred_f - jnp.mean(pred_f, axis=0, keepdims=True)
    own_slot = z * 2 + c
    pall[pl.ds(pl.multiple_of(own_slot * blk, blk), blk), :] = anom.T.astype(BF16)

    pl.semaphore_wait(barrier, nz + 1)
    for p in range(PRED_PIECES):
        send_own(pcopy, p)
    for t in range(groups):
        x = theta_ref[:, t * blk:(t + 1) * blk].astype(F32)
        th[0, t] = (x - jnp.mean(x, axis=0, keepdims=True)).astype(BF16)
        tcopy(t).start()
    for p in range(PRED_PIECES):
        pcopy(z, c, p, 2).start()

    block_of_row = lax.broadcasted_iota(jnp.int32, (nobs, blk), 0)
    for t in range(groups):
        hit = jnp.zeros((nobs, blk), F32)
        for slot in range(patt_ref.shape[1]):
            hit = jnp.where(block_of_row == patt_ref[t:t + 1, slot:slot + 1], 1.0, hit)
        mask[0, :, t * blk:(t + 1) * blk] = hit
    kcopy.start()

    column = lax.broadcasted_iota(jnp.int32, (1, blk), 1)
    usable = (column < count_ref[me]).astype(F32)
    prec = prec_ref[...]
    innov = (
        usable
        * (
            prec * (val_ref[...] - pred_ref[...].astype(F32))
            + jnp.sqrt(prec) * pert_ref[...].astype(F32)
        )
    ).astype(BF16)
    iall[:, pl.ds(pl.multiple_of(own_slot * blk, blk), blk)] = innov
    for k in range(AHEAD):
        send_own(icopy, k)
    for k in range(CHUNKS):
        icopy(z, c, k, 2).start()
    squares = jnp.square(innov.astype(F32))
    mis[0] = jnp.sum(squares.reshape(members // 8, 8, blk), axis=0)
    mcopy(0, 1, 0, sib).start()

    def cross_pair(slot, which, t):
        linked = mask[which, pl.ds((slot // 2) * 4 + y * 2 + slot % 2, 1), t * blk:(t + 1) * blk]
        rows = pl.ds(pl.multiple_of(slot * blk, blk), blk)
        found = jnp.dot(pall[rows, :], th[which, t], preferred_element_type=F32)
        at = (which * groups + t) * blk
        cross[rows, at:at + blk] = (found * linked).astype(BF16)

    def cross_own(zz):
        for p in range(PRED_PIECES):
            pcopy(zz, 1 - c, p, 2).wait_recv()

        def one(cc, _):
            for t in range(groups):
                cross_pair(zz * 2 + cc, 0, t)
            return 0

        lax.fori_loop(0, 2, one, 0)

    cross_own(z)
    for s in range(nz - 1):
        for p in range(PRED_PIECES):
            relay(pcopy, s, p)

        @pl.when(z - 1 - s >= 0)
        def _():
            cross_own(z - 1 - s)

        @pl.when(z + 1 + s < nz)
        def _():
            cross_own(z + 1 + s)

        if s == 0:
            mcopy(0, 1, 0, sib).wait_recv()
            mis[2] = mis[0] + mis[1]
            mcopy(2, 3, 1, mate).start()
        if s == 1:
            mcopy(2, 3, 1, mate).wait_recv()
            mis[4 + z] = mis[2] + mis[3]
            for h in range(1, nz):
                mcopy(4 + z, 4 + z, 1 + h, dev((z + h) % nz, y, c)).start()

    kcopy.wait_recv()
    for t in range(groups):
        tcopy(t).wait_recv()

    def mate_cross(slot, _):
        for t in range(groups):
            cross_pair(slot, 1, t)
        return 0

    lax.fori_loop(0, nz * 2, mate_cross, 0)

    for h in range(1, nz):
        other = (z + h) % nz
        mcopy(4 + other, 4 + other, 1 + h, dev(other, y, c)).wait_recv()
    tile = mis[4]
    for zz in range(1, nz):
        tile = tile + mis[4 + zz]
    misfit = jnp.sum(jnp.sum(tile, axis=0, keepdims=True), axis=1, keepdims=True)
    total = count_ref[0]
    for b in range(1, nobs):
        total = total + count_ref[b]
    scale = 1.0 / (1.0 + misfit / (members * total.astype(F32))) / (members - 1)

    def finish(k):
        ucopy(k).wait_recv()
        rows = pl.ds(pl.multiple_of(k * rk, rk), rk)
        update = own_sum[rows, :] + precv[rows, :].astype(F32)
        out_ref[rows, :] = (theta_ref[rows, :].astype(F32) + scale * update).astype(BF16)

    def chunk(k, _):
        @pl.when(k + AHEAD < CHUNKS)
        def _():
            send_own(icopy, k + AHEAD)

        for s in range(nz - 1):
            relay(icopy, s, k)
        for zz in range(nz):
            icopy(zz, 1 - c, k, 2).wait_recv()
        rows = pl.ds(pl.multiple_of(k * rk, rk), rk)
        psend[rows, :] = jnp.dot(
            iall[rows, :], cross[:, width:], preferred_element_type=F32
        ).astype(BF16)
        ucopy(k).start()
        own_sum[rows, :] = jnp.dot(
            iall[rows, :], cross[:, :width], preferred_element_type=F32
        )

        @pl.when(k >= 2)
        def _():
            finish(k - 2)

        return 0

    lax.fori_loop(0, CHUNKS, chunk, 0)
    finish(CHUNKS - 2)
    finish(CHUNKS - 1)

    def drain(copy, p):
        for zz in range(nz):
            @pl.when((z + 1 < nz) & (z >= zz))
            def _():
                copy(zz, c, p, 0).wait_send()

            @pl.when((z >= 1) & (z <= zz))
            def _():
                copy(zz, c, p, 1).wait_send()

            copy(zz, c, p, 2).wait_send()

    for p in range(PRED_PIECES):
        drain(pcopy, p)

    def drain_chunk(k, _):
        drain(icopy, k)
        ucopy(k).wait_send()
        return 0

    lax.fori_loop(0, CHUNKS, drain_chunk, 0)
    for t in range(groups):
        tcopy(t).wait_send()
    kcopy.wait_send()
    mcopy(0, 1, 0, sib).wait_send()
    mcopy(2, 3, 1, mate).wait_send()
    for h in range(1, nz):
        mcopy(4 + z, 4 + z, 1 + h, dev((z + h) % nz, y, c)).wait_send()


def body(theta, predictions, perturb, obs_value, obs_prec, pattern, obs_count):
    members, width = theta.shape
    blk = predictions.shape[1]
    groups = width // blk
    nobs = lax.axis_size("obs")
    nz = nobs // 4
    row = nz * 2
    dma = pltpu.SemaphoreType.DMA
    vmem = pl.BlockSpec(memory_space=pltpu.VMEM)
    return pl.pallas_call(
        functools.partial(kernel, nz),
        out_shape=jax.ShapeDtypeStruct((members, width), BF16),
        in_specs=[vmem] * 6 + [pl.BlockSpec(memory_space=pltpu.SMEM)],
        out_specs=vmem,
        scratch_shapes=[
            pltpu.VMEM((2, groups, members, blk), BF16),
            pltpu.VMEM((row * blk, members), BF16),
            pltpu.VMEM((members, row * blk), BF16),
            pltpu.VMEM((row * blk, 2 * width), BF16),
            pltpu.VMEM((members, width), F32),
            pltpu.VMEM((members, width), BF16),
            pltpu.VMEM((members, width), BF16),
            pltpu.VMEM((2, nobs, width), F32),
            pltpu.VMEM((4 + nz, 8, blk), F32),
            dma((3, PRED_PIECES, nz)),
            dma((PRED_PIECES, row)),
            dma((3, CHUNKS, nz)),
            dma((CHUNKS, row)),
            dma((groups,)),
            dma((groups,)),
            dma(()),
            dma(()),
            dma((1 + nz,)),
            dma((4 + nz,)),
            dma((CHUNKS,)),
            dma((CHUNKS,)),
        ],
        compiler_params=pltpu.CompilerParams(
            collective_id=0, has_side_effects=True, vmem_limit_bytes=58 * 1024 * 1024
        ),
        cost_estimate=pl.CostEstimate(
            flops=4 * members * nobs * blk * width,
            bytes_accessed=2 * members * (2 * width + 2 * blk),
            transcendentals=0,
        ),
    )(
        theta, predictions, perturb,
        obs_value.reshape(1, blk), obs_prec.reshape(1, blk), pattern, obs_count,
    )


def solution(mesh):
    return jax.shard_map(
        body,
        mesh=mesh,
        in_specs=(
            P(None, ("parts", "obs")),
            P(None, ("parts", "obs")),
            P(None, ("parts", "obs")),
            P(("parts", "obs")),
            P(("parts", "obs")),
            P(("parts", "obs"), None),
            P("parts"),
        ),
        out_specs=P(None, ("parts", "obs")),
        check_vma=False,
    )
```

```python
import functools
import jax
import jax.numpy as jnp
from jax import lax
from jax.experimental import pallas as pl
from jax.experimental.pallas import tpu as pltpu
from jax.sharding import PartitionSpec as P

MESH = pl.DeviceIdType.MESH
F32 = jnp.float32
BF16 = jnp.bfloat16
PRED_PIECES = 2
CHUNKS = 4
AHEAD = 2


def kernel(
    nz,
    theta_ref, pred_ref, pert_ref, val_ref, prec_ref, patt_ref, count_ref,
    out_ref,
    th, pall, iall, cross, own_sum, psend, precv, mask, mis,
    ps, pr, isd, ir, ts, tr, ks, kr, ms, mr, us, ur,
):
    members, width = theta_ref.shape
    blk = pred_ref.shape[1]
    groups = width // blk
    nobs = nz * 4
    rp = blk // PRED_PIECES
    rk = members // CHUNKS
    part = lax.axis_index("parts")
    me = lax.axis_index("obs")
    z = me // 4
    y = (me // 2) % 2
    c = me % 2

    def dev(zz, yy, cc):
        return (part, zz * 4 + yy * 2 + cc)

    sib = dev(z, y, 1 - c)
    mate = dev(z, 1 - y, c)

    barrier = pltpu.get_barrier_semaphore()
    pl.semaphore_signal(barrier, inc=1, device_id=sib, device_id_type=MESH)
    pl.semaphore_signal(barrier, inc=1, device_id=mate, device_id_type=MESH)
    for h in range(1, nz):
        pl.semaphore_signal(
            barrier, inc=1, device_id=dev((z + h) % nz, y, c), device_id_type=MESH
        )

    def target(d):
        return (dev(z + 1, y, c), dev(z - 1, y, c), sib)[d]

    def pcopy(zz, cc, p, d):
        r = pall.at[pl.ds(pl.multiple_of((zz * 2 + cc) * blk + p * rp, rp), rp), :]
        return pltpu.make_async_remote_copy(
            src_ref=r, dst_ref=r, send_sem=ps.at[d, p, zz], recv_sem=pr.at[p, zz * 2 + cc],
            device_id=target(d), device_id_type=MESH,
        )

    def icopy(zz, cc, k, d):
        r = iall.at[
            pl.ds(pl.multiple_of(k * rk, rk), rk),
            pl.ds(pl.multiple_of((zz * 2 + cc) * blk, blk), blk),
        ]
        return pltpu.make_async_remote_copy(
            src_ref=r, dst_ref=r, send_sem=isd.at[d, k, zz], recv_sem=ir.at[k, zz * 2 + cc],
            device_id=target(d), device_id_type=MESH,
        )

    def send_own(copy, p):
        @pl.when(z + 1 < nz)
        def _():
            copy(z, c, p, 0).start()

        @pl.when(z >= 1)
        def _():
            copy(z, c, p, 1).start()

    def relay(copy, s, p):
        below = z - 1 - s
        above = z + 1 + s

        @pl.when(below >= 0)
        def _():
            copy(below, c, p, 2).wait_recv()

            @pl.when(z + 1 < nz)
            def _():
                copy(below, c, p, 0).start()

            copy(below, c, p, 2).start()

        @pl.when(above < nz)
        def _():
            copy(above, c, p, 2).wait_recv()

            @pl.when(z >= 1)
            def _():
                copy(above, c, p, 1).start()

            copy(above, c, p, 2).start()

    def tcopy(t):
        return pltpu.make_async_remote_copy(
            src_ref=th.at[0, t], dst_ref=th.at[1, t], send_sem=ts.at[t], recv_sem=tr.at[t],
            device_id=mate, device_id_type=MESH,
        )

    kcopy = pltpu.make_async_remote_copy(
        src_ref=mask.at[0], dst_ref=mask.at[1], send_sem=ks, recv_sem=kr,
        device_id=mate, device_id_type=MESH,
    )

    def ucopy(k):
        rows = pl.ds(pl.multiple_of(k * rk, rk), rk)
        return pltpu.make_async_remote_copy(
            src_ref=psend.at[rows, :], dst_ref=precv.at[rows, :],
            send_sem=us.at[k], recv_sem=ur.at[k], device_id=mate, device_id_type=MESH,
        )

    def mcopy(src, dst, sem, device):
        return pltpu.make_async_remote_copy(
            src_ref=mis.at[src], dst_ref=mis.at[dst], send_sem=ms.at[sem], recv_sem=mr.at[dst],
            device_id=device, device_id_type=MESH,
        )

    pred_f = pred_ref[...].astype(F32)
    anom = pred_f - jnp.mean(pred_f, axis=0, keepdims=True)
    own_slot = z * 2 + c
    pall[pl.ds(pl.multiple_of(own_slot * blk, blk), blk), :] = anom.T.astype(BF16)

    pl.semaphore_wait(barrier, nz + 1)
    for p in range(PRED_PIECES):
        send_own(pcopy, p)
    for t in range(groups):
        x = theta_ref[:, t * blk:(t + 1) * blk].astype(F32)
        th[0, t] = (x - jnp.mean(x, axis=0, keepdims=True)).astype(BF16)
        tcopy(t).start()
    for p in range(PRED_PIECES):
        pcopy(z, c, p, 2).start()

    block_of_row = lax.broadcasted_iota(jnp.int32, (nobs, blk), 0)
    for t in range(groups):
        hit = jnp.zeros((nobs, blk), F32)
        for slot in range(patt_ref.shape[1]):
            hit = jnp.where(block_of_row == patt_ref[t:t + 1, slot:slot + 1], 1.0, hit)
        mask[0, :, t * blk:(t + 1) * blk] = hit
    kcopy.start()

    column = lax.broadcasted_iota(jnp.int32, (1, blk), 1)
    usable = (column < count_ref[me]).astype(F32)
    prec = prec_ref[...]
    innov = (
        usable
        * (
            prec * (val_ref[...] - pred_ref[...].astype(F32))
            + jnp.sqrt(prec) * pert_ref[...].astype(F32)
        )
    ).astype(BF16)
    iall[:, pl.ds(pl.multiple_of(own_slot * blk, blk), blk)] = innov
    for k in range(AHEAD):
        send_own(icopy, k)
    for k in range(CHUNKS):
        icopy(z, c, k, 2).start()
    squares = jnp.square(innov.astype(F32))
    mis[0] = jnp.sum(squares.reshape(members // 8, 8, blk), axis=0)
    mcopy(0, 1, 0, sib).start()

    def cross_pair(slot, which, t):
        linked = mask[which, pl.ds((slot // 2) * 4 + y * 2 + slot % 2, 1), t * blk:(t + 1) * blk]
        rows = pl.ds(pl.multiple_of(slot * blk, blk), blk)
        found = jnp.dot(pall[rows, :], th[which, t], preferred_element_type=F32)
        at = (which * groups + t) * blk
        cross[rows, at:at + blk] = (found * linked).astype(BF16)

    def cross_own(zz):
        for p in range(PRED_PIECES):
            pcopy(zz, 1 - c, p, 2).wait_recv()

        def one(cc, _):
            for t in range(groups):
                cross_pair(zz * 2 + cc, 0, t)
            return 0

        lax.fori_loop(0, 2, one, 0)

    cross_own(z)
    for s in range(nz - 1):
        for p in range(PRED_PIECES):
            relay(pcopy, s, p)

        @pl.when(z - 1 - s >= 0)
        def _():
            cross_own(z - 1 - s)

        @pl.when(z + 1 + s < nz)
        def _():
            cross_own(z + 1 + s)

        if s == 0:
            mcopy(0, 1, 0, sib).wait_recv()
            mis[2] = mis[0] + mis[1]
            mcopy(2, 3, 1, mate).start()
        if s == 1:
            mcopy(2, 3, 1, mate).wait_recv()
            mis[4 + z] = mis[2] + mis[3]
            for h in range(1, nz):
                mcopy(4 + z, 4 + z, 1 + h, dev((z + h) % nz, y, c)).start()

    relay(icopy, 0, 0)
    kcopy.wait_recv()
    for t in range(groups):
        tcopy(t).wait_recv()

    def mate_cross(slot, _):
        for t in range(groups):
            cross_pair(slot, 1, t)
        return 0

    lax.fori_loop(0, nz * 2, mate_cross, 0)

    for h in range(1, nz):
        other = (z + h) % nz
        mcopy(4 + other, 4 + other, 1 + h, dev(other, y, c)).wait_recv()
    tile = mis[4]
    for zz in range(1, nz):
        tile = tile + mis[4 + zz]
    misfit = jnp.sum(jnp.sum(tile, axis=0, keepdims=True), axis=1, keepdims=True)
    total = count_ref[0]
    for b in range(1, nobs):
        total = total + count_ref[b]
    scale = 1.0 / (1.0 + misfit / (members * total.astype(F32))) / (members - 1)

    def finish(k):
        ucopy(k).wait_recv()
        rows = pl.ds(pl.multiple_of(k * rk, rk), rk)
        update = own_sum[rows, :] + precv[rows, :].astype(F32)
        out_ref[rows, :] = (theta_ref[rows, :].astype(F32) + scale * update).astype(BF16)

    def chunk(k, _):
        @pl.when(k + AHEAD < CHUNKS)
        def _():
            send_own(icopy, k + AHEAD)

        for s in range(1, nz - 1):
            relay(icopy, s, k)

        @pl.when(k + 1 < CHUNKS)
        def _():
            relay(icopy, 0, k + 1)

        for zz in range(nz):
            icopy(zz, 1 - c, k, 2).wait_recv()
        rows = pl.ds(pl.multiple_of(k * rk, rk), rk)
        psend[rows, :] = jnp.dot(
            iall[rows, :], cross[:, width:], preferred_element_type=F32
        ).astype(BF16)
        ucopy(k).start()
        own_sum[rows, :] = jnp.dot(
            iall[rows, :], cross[:, :width], preferred_element_type=F32
        )

        @pl.when(k >= 2)
        def _():
            finish(k - 2)

        return 0

    lax.fori_loop(0, CHUNKS, chunk, 0)
    finish(CHUNKS - 2)
    finish(CHUNKS - 1)

    def drain(copy, p):
        for zz in range(nz):
            @pl.when((z + 1 < nz) & (z >= zz))
            def _():
                copy(zz, c, p, 0).wait_send()

            @pl.when((z >= 1) & (z <= zz))
            def _():
                copy(zz, c, p, 1).wait_send()

            copy(zz, c, p, 2).wait_send()

    for p in range(PRED_PIECES):
        drain(pcopy, p)

    def drain_chunk(k, _):
        drain(icopy, k)
        ucopy(k).wait_send()
        return 0

    lax.fori_loop(0, CHUNKS, drain_chunk, 0)
    for t in range(groups):
        tcopy(t).wait_send()
    kcopy.wait_send()
    mcopy(0, 1, 0, sib).wait_send()
    mcopy(2, 3, 1, mate).wait_send()
    for h in range(1, nz):
        mcopy(4 + z, 4 + z, 1 + h, dev((z + h) % nz, y, c)).wait_send()


def body(theta, predictions, perturb, obs_value, obs_prec, pattern, obs_count):
    members, width = theta.shape
    blk = predictions.shape[1]
    groups = width // blk
    nobs = lax.axis_size("obs")
    nz = nobs // 4
    row = nz * 2
    dma = pltpu.SemaphoreType.DMA
    vmem = pl.BlockSpec(memory_space=pltpu.VMEM)
    return pl.pallas_call(
        functools.partial(kernel, nz),
        out_shape=jax.ShapeDtypeStruct((members, width), BF16),
        in_specs=[vmem] * 6 + [pl.BlockSpec(memory_space=pltpu.SMEM)],
        out_specs=vmem,
        scratch_shapes=[
            pltpu.VMEM((2, groups, members, blk), BF16),
            pltpu.VMEM((row * blk, members), BF16),
            pltpu.VMEM((members, row * blk), BF16),
            pltpu.VMEM((row * blk, 2 * width), BF16),
            pltpu.VMEM((members, width), F32),
            pltpu.VMEM((members, width), BF16),
            pltpu.VMEM((members, width), BF16),
            pltpu.VMEM((2, nobs, width), F32),
            pltpu.VMEM((4 + nz, 8, blk), F32),
            dma((3, PRED_PIECES, nz)),
            dma((PRED_PIECES, row)),
            dma((3, CHUNKS, nz)),
            dma((CHUNKS, row)),
            dma((groups,)),
            dma((groups,)),
            dma(()),
            dma(()),
            dma((1 + nz,)),
            dma((4 + nz,)),
            dma((CHUNKS,)),
            dma((CHUNKS,)),
        ],
        compiler_params=pltpu.CompilerParams(
            collective_id=0, has_side_effects=True, vmem_limit_bytes=58 * 1024 * 1024
        ),
        cost_estimate=pl.CostEstimate(
            flops=4 * members * nobs * blk * width,
            bytes_accessed=2 * members * (2 * width + 2 * blk),
            transcendentals=0,
        ),
    )(
        theta, predictions, perturb,
        obs_value.reshape(1, blk), obs_prec.reshape(1, blk), pattern, obs_count,
    )


def solution(mesh):
    return jax.shard_map(
        body,
        mesh=mesh,
        in_specs=(
            P(None, ("parts", "obs")),
            P(None, ("parts", "obs")),
            P(None, ("parts", "obs")),
            P(("parts", "obs")),
            P(("parts", "obs")),
            P(("parts", "obs"), None),
            P("parts"),
        ),
        out_specs=P(None, ("parts", "obs")),
        check_vma=False,
    )
```
